1024 devices in a mesh: dp: 16 (over z), expert: 64 (over y, x, core).
Axes of the slice: x: 4, y: 8, z: 16, core: 2. Of those that a mesh axis runs over, the one named last changes fastest.
Arguments:
- tokens: bfloat16 [8192, 3584], P('expert', 'dp'), may hold values from -6 to 6
- cotangent: bfloat16 [8192, 3584], P('expert', 'dp'), may hold values from -1.1953125 to 1.1953125
- expert_ids: int32 [8192, 2], P('expert'), may hold values from 0 to 63, all different within a row; in each aligned block of 128 rows (0 to 127, 128 to 255, ...) at most 5 rows name the same one
- combine: float32 [8192, 2], P('expert'), may hold values from 0.2 to 1
- w_up: bfloat16 [64, 3584, 2432], P('expert', 'dp'), may hold values from -0.09375 to 0.09375
- w_down: bfloat16 [64, 2432, 3584], P('expert', None, 'dp'), may hold values from -0.125 to 0.125
Outputs:
- layer_out: bfloat16 [8192, 3584], P('expert', 'dp')
- input_grad: bfloat16 [8192, 3584], P('expert', 'dp')
- combine_grad: float32 [8192, 2], P('expert')
- down_grad: bfloat16 [64, 2432, 3584], P('expert', None, 'dp')
The draws below stay inside these ranges and needn't reach their ends.
Inputs may be any that keep to these rules, and one draw needn't show every extreme that they name: `expert_ids`: the two ids of a token differ. Among the 256 ids of one index s of expert (tokens s * 128 to (s + 1) * 128 - 1), no expert appears more than 5 times, and some expert appears exactly 5 times.
All inputs are finite; a program needn't handle non-finite values.
Results may differ from the reference program's by a relative error of at most 0.029.
Values may be sent and summed in bfloat16 or wider, within the bound.
No kernel may reach another device: no remote copies, remote signals or barrier semaphores. Data moves between devices by JAX's collectives and lax.ppermute only.
A program may use at most 32 MiB of HBM per device.

```python
import math
import jax
import jax.numpy as jnp
import numpy as np
from jax import lax

D = 3584
FF = 2432
TOK_DEV = 128
EXPERTS = 64
TOKENS = 8192
CAP = 5
FEAT = 224
N_DP = 16
N_EXPERT = 64


def shard_levels(own_key, dims, split, low, top_value):
    def one(dim, parts):
        steps = jax.random.uniform(jax.random.fold_in(jax.random.fold_in(own_key, 6), dim), (parts,), jnp.float32, low / len(split), top_value / len(split))
        return jnp.repeat(jnp.exp(steps), dims[dim] // parts).reshape((-1,) + (1,) * (len(dims) - dim - 1))

    factor_of = one(*split[0])
    for cut in split[1:]:
        factor_of = factor_of * one(*cut)
    return factor_of


def shared_out(key, own, number, rows, number_of, top, limit, lean):
    sequence = jax.random.permutation(key, number_of)
    heavy_load, ordinary = portions_of(number_of, rows * top, limit, lean, True), portions_of(number_of, rows * top, limit, lean, False)
    places = jnp.arange(number_of)

    def named(sizes, turn):
        used = int((sizes > 0).sum())
        fixed = max(1, used // 4)
        shifted = fixed + (places - fixed + turn * (used - fixed)) % max(1, number_of - fixed)
        return jnp.zeros((number_of,), jnp.int32).at[sequence[jnp.where(places < fixed, places, shifted)]].set(jnp.asarray(sizes, jnp.int32))

    sizes = jnp.where(number % 4 == 0, named(heavy_load, number // 4), named(ordinary, number - number // 4 - 1))
    mixed = jax.random.permutation(jax.random.fold_in(own, 3), number_of)
    donor, sink = mixed[0:number_of // 2 * 2:2], mixed[1:number_of // 2 * 2:2]
    margin = jnp.minimum(sizes[donor] - 1, limit - sizes[sink]) // 2
    margin = jnp.where((donor == sequence[0]) | (sink == sequence[0]) | (sizes[sink] == 0), 0, jnp.maximum(margin, 0))
    shifted = jax.random.randint(jax.random.fold_in(own, 4), (number_of // 2,), 0, 1 << 20) % (margin + 1)
    sizes = sizes.at[donor].add(-shifted).at[sink].add(shifted)
    items = jnp.searchsorted(jnp.cumsum(sizes), jnp.arange(rows * top), side="right").astype(jnp.int32)
    grid = items.reshape(top, rows).T
    grid = grid[jax.random.permutation(jax.random.fold_in(own, 1), rows)]
    turn = jax.random.randint(jax.random.fold_in(own, 2), (rows, 1), 0, top)
    return jnp.take_along_axis(grid, (jnp.arange(top)[None, :] + turn) % top, axis=1)


def portions_of(amount, total, most, slope, full):
    loads = [(1 << 20) // math.isqrt(grade ** slope) + 1 for grade in range(1, amount + 1)]
    largest = most if full else min(most, max(-(-total // amount), total * loads[0] // sum(loads)))
    least = 1 if total - largest >= amount - 1 else 0
    given, surplus = [largest] + [least] * (amount - 1), total - largest - least * (amount - 1)
    while surplus > 0:
        free = [i for i in range(1, amount) if given[i] < largest] or [i for i in range(1, amount) if given[i] < most]
        whole, remaining = sum([loads[i] for i in free]), surplus
        for i in free:
            addition = min(most - given[i], max(1, remaining * loads[i] // whole), surplus)
            given[i] = given[i] + addition
            surplus = surplus - addition
    return np.array(given)


def centred(stream_key, extent, deviation, reach, split=(), held_as=jnp.bfloat16):
    result = jax.random.normal(stream_key, extent, jnp.float32) * deviation
    if len(split) > 0:
        result = shard_levels(stream_key, extent, split, -0.22, 0.18) * result
    return jnp.clip(result, min=-reach, max=reach).astype(held_as)


def setup_inputs(seed: int = 0) -> dict:
    arg_keys = jax.random.split(jax.random.key(seed), 7)
    tokens = centred(arg_keys[0], (TOKENS, D), 1.0, 6.0, ((0, 64), (1, 16)))
    cotangent = centred(arg_keys[1], (TOKENS, D), 0.2, 1.1953125, ((0, 64), (1, 16)))
    expert_ids_keys = jax.random.split(jax.random.fold_in(arg_keys[2], 1), TOKENS // TOK_DEV)
    expert_ids_turns = jax.random.permutation(jax.random.fold_in(arg_keys[2], 3), TOKENS // TOK_DEV)
    expert_ids = jax.vmap(lambda own, number: shared_out(jax.random.fold_in(arg_keys[2], 2), own, number, TOK_DEV, EXPERTS, 2, CAP, 2))(expert_ids_keys, expert_ids_turns).reshape((TOKENS, 2))
    combine = jnp.clip(0.2 + 0.8 * jax.random.uniform(arg_keys[3], (TOKENS, 2), jnp.float32) ** shard_levels(arg_keys[3], (TOKENS, 2), ((0, 64),), -0.2, 0.2), 0.2, 1.0)
    w_up = centred(arg_keys[4], (EXPERTS, D, FF), D ** -0.5, 0.09375, ((0, 64), (1, 16)))
    w_down = centred(arg_keys[5], (EXPERTS, FF, D), FF ** -0.5, 0.125, ((0, 64), (2, 16)))
    return {"tokens": tokens, "cotangent": cotangent, "expert_ids": expert_ids, "combine": combine, "w_up": w_up, "w_down": w_down}


def silu_slope(hidden):
    sigmoid_v = jax.nn.sigmoid(hidden)
    return sigmoid_v * (1.0 + hidden * (1.0 - sigmoid_v))


def build_slots(expert_ids):
    flat_ids = expert_ids.reshape(N_EXPERT, TOK_DEV * 2)
    onehot = (flat_ids[:, :, None] == jnp.arange(EXPERTS, dtype=jnp.int32)[None, None, :]).astype(jnp.int32)
    before = jnp.cumsum(onehot, axis=1) - onehot
    position = jnp.sum(before * onehot, axis=2).astype(jnp.int32)
    source = jnp.broadcast_to(jnp.arange(N_EXPERT, dtype=jnp.int32)[:, None], flat_ids.shape)
    slot_ids = jnp.arange(N_EXPERT * TOK_DEV * 2, dtype=jnp.int32).reshape(flat_ids.shape)
    placed = jnp.full((EXPERTS, N_EXPERT, CAP), -1, jnp.int32)
    return placed.at[flat_ids, source, position].set(slot_ids)


def group_sum(partial_value):
    rounded = lax.optimization_barrier(partial_value.astype(jnp.bfloat16))
    return jnp.sum(rounded.astype(jnp.float32), axis=0)


def reference(tokens, cotangent, expert_ids, combine, w_up, w_down):
    placed = build_slots(expert_ids)
    combine_flat = combine.reshape(-1)

    def one_expert(operands):
        entries, up_block, down_block = operands
        indices = entries.reshape(-1)
        present = indices >= 0
        token_index = jnp.where(present, indices // 2, 0).astype(jnp.int32)
        slot_index = jnp.where(present, indices, 0).astype(jnp.int32)
        row_count = indices.shape[0]
        x_rows = jnp.where(present[:, None], tokens[token_index], jnp.zeros((), jnp.bfloat16))
        scaled = combine_flat[slot_index][:, None] * cotangent[token_index].astype(jnp.float32)
        scaled = jnp.where(present[:, None], scaled, jnp.float32(0.0)).astype(jnp.bfloat16)
        x_split = x_rows.astype(jnp.float32).reshape(row_count, N_DP, FEAT)
        up_split = up_block.astype(jnp.float32).reshape(N_DP, FEAT, FF)
        hidden = group_sum(jnp.einsum('rgd,gdf->grf', x_split, up_split, precision=lax.Precision.HIGHEST))
        active = jax.nn.silu(hidden).astype(jnp.bfloat16)
        y_rows = jnp.dot(active, down_block, preferred_element_type=jnp.float32).astype(jnp.bfloat16)
        g_split = scaled.astype(jnp.float32).reshape(row_count, N_DP, FEAT)
        down_split = down_block.astype(jnp.float32).reshape(FF, N_DP, FEAT)
        d_active = group_sum(jnp.einsum('rgd,fgd->grf', g_split, down_split, precision=lax.Precision.HIGHEST))
        d_hidden = (d_active * silu_slope(hidden)).astype(jnp.bfloat16)
        dx_rows = jnp.dot(d_hidden, up_block.T, preferred_element_type=jnp.float32).astype(jnp.bfloat16)
        grad_down = jnp.dot(active.T, scaled, preferred_element_type=jnp.float32).astype(jnp.bfloat16)
        return y_rows, dx_rows, grad_down

    y_all, dx_all, down_grad = lax.map(one_expert, (placed, w_up, w_down))
    flat_slots = placed.reshape(-1)
    target = jnp.where(flat_slots >= 0, flat_slots, TOKENS * 2).astype(jnp.int32)
    y_slots = jnp.zeros((TOKENS * 2, D), jnp.bfloat16).at[target].set(y_all.reshape(-1, D), mode='drop')
    dx_slots = jnp.zeros((TOKENS * 2, D), jnp.bfloat16).at[target].set(dx_all.reshape(-1, D), mode='drop')
    y_pair = y_slots.reshape(TOKENS, 2, D).astype(jnp.float32)
    dx_pair = dx_slots.reshape(TOKENS, 2, D).astype(jnp.float32)
    layer_out = (tokens.astype(jnp.float32) + combine[:, 0, None] * y_pair[:, 0] + combine[:, 1, None] * y_pair[:, 1]).astype(jnp.bfloat16)
    combine_grad = jnp.sum(y_pair * cotangent.astype(jnp.float32)[:, None, :], axis=2)
    input_grad = (cotangent.astype(jnp.float32) + dx_pair[:, 0] + dx_pair[:, 1]).astype(jnp.bfloat16)
    return layer_out, input_grad, combine_grad, down_grad
```

```python
import functools

import jax
import jax.numpy as jnp
from jax import lax
from jax.experimental import pallas as pl
from jax.experimental.pallas import tpu as pltpu
from jax.sharding import PartitionSpec as P

CAP = 5
PAD = 8
HALF = 256
F32 = jnp.float32
BF16 = jnp.bfloat16
VMEM = pl.BlockSpec(memory_space=pltpu.VMEM)
NN = (((1,), (0,)), ((), ()))
NT = (((1,), (1,)), ((), ()))
TN = (((0,), (0,)), ((), ()))


def mm(a, b, dims):
    return lax.dot_general(a, b, dims, preferred_element_type=F32)


def wide(block):
    return jnp.concatenate([block, jnp.zeros((HALF - block.shape[0], block.shape[1]), block.dtype)], axis=0)


def call(kernel, out_shape, args, scratch=(), limit=32):
    return pl.pallas_call(
        kernel,
        out_shape=out_shape,
        in_specs=[VMEM] * len(args),
        out_specs=jax.tree.map(lambda _: VMEM, out_shape),
        scratch_shapes=list(scratch),
        compiler_params=pltpu.CompilerParams(vmem_limit_bytes=limit * 1024 * 1024),
    )(*args)


def dispatch_kernel(ids_ref, comb_ref, tok_ref, cot_ref, send_ref, disp_ref):
    rows, toks = disp_ref.shape
    row = lax.broadcasted_iota(jnp.int32, (rows, toks), 0)
    row_expert = row >> 3
    row_slot = (row & 7).astype(F32)
    first = row_expert == ids_ref[0:1, :]
    second = row_expert == ids_ref[1:2, :]
    chosen = jnp.where(first | second, 1.0, 0.0)
    earlier = lax.broadcasted_iota(jnp.int32, (toks, toks), 0) < lax.broadcasted_iota(jnp.int32, (toks, toks), 1)
    before = mm(chosen.astype(BF16), jnp.where(earlier, 1.0, 0.0).astype(BF16), NN)
    here = jnp.where(before == row_slot, chosen, 0.0)
    weight = jnp.sum(here * jnp.where(first, comb_ref[0:1, :], comb_ref[1:2, :]), axis=1, keepdims=True)
    disp = here.astype(BF16)
    disp_ref[...] = disp
    send_ref[:, :HALF] = mm(disp, wide(tok_ref[...]), NT).astype(BF16)
    send_ref[:, HALF:] = (weight * mm(disp, wide(cot_ref[...]), NT)).astype(BF16)


def up_kernel(count, recv_ref, up_ref, down_ref, g_ref, *pieces):
    feat, hidden = up_ref.shape
    kept, padded = g_ref.shape[0], recv_ref.shape[0]
    row = lax.broadcasted_iota(jnp.int32, (kept, padded), 0)
    source = (row * 13108) >> 16
    wanted = source * PAD + (row - source * CAP)
    pick = jnp.where(lax.broadcasted_iota(jnp.int32, (kept, padded), 1) == wanted, 1.0, 0.0).astype(BF16)
    x_rows = mm(pick, recv_ref[:, :HALF], NN).astype(BF16)[:, :feat]
    g_rows = mm(pick, recv_ref[:, HALF:], NN).astype(BF16)[:, :feat]
    g_ref[...] = g_rows
    for rows, w_ref, outs in ((x_rows, up_ref, pieces[:count]), (g_rows, down_ref, pieces[count:])):
        for at in range(0, hidden, 256):
            cols = slice(at, min(at + 256, hidden))
            term = mm(rows, w_ref[:, cols], NN).astype(BF16)
            for i, out in enumerate(outs):
                out[:, cols] = term[8 * i : 8 * i + 8]


def down_kernel(count, *refs):
    hid, dact = refs[:count], refs[count : 2 * count]
    up_ref, down_ref, send_ref, act_ref, dhid_ref, dots_ref = refs[2 * count :]
    kept, padded = act_ref.shape[0], send_ref.shape[0]
    feat = up_ref.shape[0]
    for i in range(0, count, 2):
        h = jnp.concatenate([hid[i][...].astype(F32), hid[i + 1][...].astype(F32)], axis=0)
        d = jnp.concatenate([dact[i][...].astype(F32), dact[i + 1][...].astype(F32)], axis=0)
        s = 1.0 / (1.0 + jnp.exp(-h))
        act = (h * s).astype(BF16)
        rows = slice(8 * i, 8 * i + 16)
        act_ref[rows, :] = act
        dhid_ref[rows, :] = (d * (s * (1.0 + h * (1.0 - s)))).astype(BF16)
        dots_ref[rows, :] = jnp.broadcast_to(jnp.sum(act.astype(F32) * d, axis=1, keepdims=True), (16, HALF))
    y = mm(act_ref[...], wide(down_ref[...]), NT).astype(BF16)
    dx = mm(dhid_ref[...], wide(up_ref[...]), NT).astype(BF16)
    dots = dots_ref[...]
    high = dots.astype(BF16).astype(F32)
    lane = lax.broadcasted_iota(jnp.int32, (kept, HALF), 1)
    y = jnp.where(lane == feat, high, jnp.where(lane == feat + 1, dots - high, y.astype(F32))).astype(BF16)
    row = lax.broadcasted_iota(jnp.int32, (padded, kept), 0)
    slot = row & 7
    wanted = jnp.where(slot < CAP, (row >> 3) * CAP + slot, -1)
    place = jnp.where(lax.broadcasted_iota(jnp.int32, (padded, kept), 1) == wanted, 1.0, 0.0).astype(BF16)
    send_ref[:, :HALF] = mm(place, y, NN).astype(BF16)
    send_ref[:, HALF:] = mm(place, dx, NN).astype(BF16)


def grad_kernel(g_ref, act_ref, out_ref):
    hidden = act_ref.shape[1]
    for at in range(0, hidden, 256):
        cols = slice(at, min(at + 256, hidden))
        out_ref[:, cols] = mm(g_ref[...], act_ref[:, cols], TN).astype(BF16)


def combine_kernel(recv_ref, disp_ref, ids_ref, comb_ref, tok_ref, cot_ref, out_ref, dx_ref, grad_ref):
    rows, toks = disp_ref.shape
    feat = tok_ref.shape[0]
    row_expert = lax.broadcasted_iota(jnp.int32, (rows, toks), 0) >> 3
    disp = disp_ref[...].astype(F32)
    total = tok_ref[...].astype(F32)
    for k in range(2):
        mine = jnp.where(row_expert == ids_ref[k : k + 1, :], disp, 0.0).astype(BF16)
        y = mm(recv_ref[:, :HALF], mine, TN)
        weight = comb_ref[k : k + 1, :]
        total = total + weight * y[:feat]
        grad_ref[k : k + 1, :] = (y[feat : feat + 1] + y[feat + 1 : feat + 2]) / weight
    out_ref[...] = total.astype(BF16)
    dx = mm(recv_ref[:, HALF:], disp_ref[...], TN)
    dx_ref[...] = (cot_ref[...].astype(F32) + dx[:feat]).astype(BF16)


def exchange(rows, groups):
    parts = rows.reshape(groups, PAD, 2 * HALF)
    parts = lax.all_to_all(parts, "expert", split_axis=0, concat_axis=0, tiled=True)
    return parts.reshape(groups * PAD, 2 * HALF)


def body(tokens, cotangent, expert_ids, combine, w_up, w_down):
    toks, feat = tokens.shape
    groups = lax.axis_size("expert")
    hidden = w_up.shape[2]
    kept, padded = groups * CAP, groups * PAD
    count = kept // 8
    shape = jax.ShapeDtypeStruct
    tok, cot, ids, comb = tokens.T, cotangent.T, expert_ids.T, combine.T
    up, down = w_up[0], w_down[0].T

    send, disp = call(
        dispatch_kernel, (shape((padded, 2 * HALF), BF16), shape((padded, toks), BF16)), (ids, comb, tok, cot)
    )
    recv = exchange(send, groups)
    g_rows, *terms = call(
        functools.partial(up_kernel, count),
        (shape((kept, feat), BF16),) + (shape((8, hidden), BF16),) * (2 * count),
        (recv, up, down),
    )
    sums = lax.psum(tuple(terms), "dp")
    send_back, act = call(
        functools.partial(down_kernel, count),
        (shape((padded, 2 * HALF), BF16), shape((kept, hidden), BF16)),
        (*sums, up, down),
        [pltpu.VMEM((kept, hidden), BF16), pltpu.VMEM((kept, HALF), F32)],
    )
    back = exchange(send_back, groups)
    down_grad = call(grad_kernel, shape((feat, hidden), BF16), (g_rows, act))
    layer_out, input_grad, combine_grad = call(
        combine_kernel,
        (shape((feat, toks), BF16), shape((feat, toks), BF16), shape((2, toks), F32)),
        (back, disp, ids, comb, tok, cot),
    )
    return layer_out.T, input_grad.T, combine_grad.T, down_grad.T[None]


def solution(mesh):
    in_specs = (
        P("expert", "dp"),
        P("expert", "dp"),
        P("expert", None),
        P("expert", None),
        P("expert", "dp", None),
        P("expert", None, "dp"),
    )
    out_specs = (P("expert", "dp"), P("expert", "dp"), P("expert", None), P("expert", None, "dp"))
    return jax.shard_map(body, mesh=mesh, in_specs=in_specs, out_specs=out_specs, check_vma=False)
```

```python
import functools

import jax
import jax.numpy as jnp
from jax import lax
from jax.experimental import pallas as pl
from jax.experimental.pallas import tpu as pltpu
from jax.sharding import PartitionSpec as P

CAP = 5
PAD = 8
TILE = 128
F32 = jnp.float32
BF16 = jnp.bfloat16
VMEM = pl.BlockSpec(memory_space=pltpu.VMEM)
HBM = pl.BlockSpec(memory_space=pltpu.HBM)
NN = (((1,), (0,)), ((), ()))
NT = (((1,), (1,)), ((), ()))
TN = (((0,), (0,)), ((), ()))


def mm(a, b, dims):
    return lax.dot_general(a, b, dims, preferred_element_type=F32)


def halves(block):
    half = block.shape[0] // 2
    zeros = jnp.zeros((TILE - half, block.shape[1]), block.dtype)
    return jnp.concatenate([block[:half], zeros, block[half:], zeros], axis=0)


def iota(shape, dim):
    return lax.broadcasted_iota(jnp.int32, shape, dim)


def ones_at(mask):
    return jnp.where(mask, 1.0, 0.0).astype(BF16)


def call(kernel, out_shape, out_specs, args, in_specs, scratch=(), limit=60):
    return pl.pallas_call(
        kernel,
        out_shape=out_shape,
        in_specs=in_specs,
        out_specs=out_specs,
        scratch_shapes=list(scratch),
        compiler_params=pltpu.CompilerParams(vmem_limit_bytes=limit * 1024 * 1024),
    )(*args)


def load(pairs, sems):
    copies = [pltpu.make_async_copy(src, dst, sems.at[i]) for i, (src, dst) in enumerate(pairs)]
    for copy in copies:
        copy.start()
    return copies


def dispatch_kernel(ids_hbm, comb_hbm, tok_hbm, cot_hbm, send_ref, disp_ref, ids_ref, comb_ref, tok_ref, cot_ref, sems):
    copies = load(((ids_hbm, ids_ref), (comb_hbm, comb_ref), (tok_hbm, tok_ref), (cot_hbm, cot_ref)), sems)
    rows, toks = send_ref.shape[0], tok_ref.shape[1]
    row = iota((rows, toks), 0)
    expert, slot = row >> 3, row & 7
    earlier = ones_at(iota((toks, toks), 0) < iota((toks, toks), 1))
    copies[0].wait()
    first = expert == ids_ref[0:1, :]
    second = expert == ids_ref[1:2, :]
    chosen = jnp.where(first | second, 1.0, 0.0)
    before = mm(chosen.astype(BF16), earlier, NN).astype(jnp.int32)
    here = [
        jnp.where(before == jnp.where(slot < CAP, slot, jnp.where(slot - shift < CAP, slot - shift, -1)), chosen, 0.0)
        for shift in (5, 2)
    ]
    copies[1].wait()
    weight = jnp.where(first, comb_ref[0:1, :], comb_ref[1:2, :])
    weights = [jnp.sum(h * weight, axis=1, keepdims=True) for h in here]
    picks = [h.astype(BF16) for h in here]
    disp_ref[:, :toks] = picks[0]
    disp_ref[:, toks:] = picks[1]
    copies[2].wait()
    copies[3].wait()
    x, g = halves(tok_ref[...]), halves(cot_ref[...])
    low = iota((rows, TILE), 0) & 7 < CAP
    for i in range(2):
        source = jnp.concatenate([x[TILE * i : TILE * i + TILE], g[TILE:]], axis=0)
        both = mm(picks[i], source, NT)
        send_ref[:, TILE * i : TILE * i + TILE] = jnp.where(low, both[:, :TILE], weights[i] * both[:, TILE:]).astype(BF16)
    send_ref[:, 2 * TILE :] = (weights[0] * mm(picks[0], g[:TILE], NT)).astype(BF16)


def spans(hidden):
    cut = (hidden // 2 + 127) // 128 * 128
    return (0, cut), (cut, hidden)


def pieces_of(refs, kept, hidden):
    places = [(slice(r, r + 16), slice(*span)) for r in range(0, kept, 16) for span in spans(hidden)]
    return [(ref, *place) for ref, place in zip(refs, places, strict=True)]


def up_kernel(count, recv_ref, up_hbm, down_hbm, g_ref, *refs):
    outs, (term_ref, up_ref, down_ref, in_sems, out_sems) = refs[: 2 * count], refs[2 * count :]
    copies = load(((up_hbm, up_ref), (down_hbm, down_ref)), in_sems)
    feat, hidden = up_ref.shape
    half = feat // 2
    kept, padded = g_ref.shape[0], recv_ref.shape[0]
    row = iota((kept, padded), 0)
    source = (row * 13108) >> 16
    slot = row - source * CAP
    at = iota((kept, padded), 1) - source * PAD
    main = mm(ones_at(at == slot), recv_ref[...], NN)
    extra = mm(ones_at(at == jnp.where(slot < 3, slot + 5, padded)), recv_ref[:, :TILE], NN)
    extra += mm(ones_at(at == jnp.where(slot < 3, padded, slot + 2)), recv_ref[:, TILE : 2 * TILE], NN)
    x_rows = jnp.concatenate([main[:, :half], main[:, TILE : TILE + half]], axis=1).astype(BF16)
    g_rows = jnp.concatenate([main[:, 2 * TILE : 2 * TILE + half], extra[:, :half]], axis=1).astype(BF16)
    g_ref[...] = g_rows
    started = []
    for k, (rows, w_ref) in enumerate(((x_rows, up_ref), (g_rows, down_ref))):
        copies[k].wait()
        for at in range(0, hidden, 256):
            cols = slice(at, min(at + 256, hidden))
            term_ref[k, :, cols] = mm(rows, w_ref[:, cols], NN).astype(BF16)
        for i, (out, r, c) in enumerate(pieces_of(outs[k * count : (k + 1) * count], kept, hidden)):
            copy = pltpu.make_async_copy(term_ref.at[k, r, c], out, out_sems.at[k * count + i])
            copy.start()
            started.append(copy)
    for copy in started:
        copy.wait()


def down_kernel(count, *refs):
    sums, (up_hbm, down_hbm) = refs[: 2 * count], refs[2 * count : 2 * count + 2]
    send_ref, act_hbm, sum_ref, act_ref, dhid_ref, dots_ref, up_ref, down_ref, sems, w_sems = refs[2 * count + 2 :]
    kept, hidden = act_ref.shape
    padded, feat = send_ref.shape[0], up_ref.shape[0]
    half = feat // 2
    hid = pieces_of(sums[:count], kept, hidden)
    dact = pieces_of(sums[count:], kept, hidden)
    waits = []
    for i in range(count):
        for k, (ref, r, c) in enumerate((hid[i], dact[i])):
            copy = pltpu.make_async_copy(ref, sum_ref.at[k, r, c], sems.at[k * count + i])
            copy.start()
            waits.append(copy)
    copies = load(((up_hbm, up_ref), (down_hbm, down_ref)), w_sems)
    for i in range(0, count, 2):
        for copy in waits[2 * i : 2 * i + 4]:
            copy.wait()
        rows = hid[i][1]
        h = sum_ref[0, rows, :].astype(F32)
        d = sum_ref[1, rows, :].astype(F32)
        s = 1.0 / (1.0 + jnp.exp(-h))
        act = (h * s).astype(BF16)
        act_ref[rows, :] = act
        dhid_ref[rows, :] = (d * (s * (1.0 + h * (1.0 - s)))).astype(BF16)
        dots_ref[rows, :] = jnp.broadcast_to(jnp.sum(act.astype(F32) * d, axis=1, keepdims=True), (16, TILE))
    act_copy = pltpu.make_async_copy(act_ref, act_hbm, w_sems.at[2])
    act_copy.start()
    row = iota((padded, kept), 0)
    slot = row & 7
    at = iota((padded, kept), 1) - (row >> 3) * CAP
    base = ones_at((at == slot) & (slot < CAP))
    copies[1].wait()
    y = mm(act_ref[...], halves(down_ref[...]), NT).astype(BF16)
    dots = dots_ref[...]
    high = dots.astype(BF16).astype(F32)
    lane = iota((kept, TILE), 1)
    low = jnp.where(lane == half, high, jnp.where(lane == half + 1, dots - high, y[:, :TILE].astype(F32))).astype(BF16)
    copies[0].wait()
    dx = mm(dhid_ref[...], halves(up_ref[...]), NT).astype(BF16)
    for i, (part, shift) in enumerate(((low, 5), (y[:, TILE:], 2))):
        lift = ones_at((slot >= CAP) & (slot - shift < (3 if i == 0 else CAP)) & (at == slot - shift))
        tile = mm(base, part, NN) + mm(lift, dx[:, TILE:], NN)
        send_ref[:, TILE * i : TILE * i + TILE] = tile.astype(BF16)
    send_ref[:, 2 * TILE :] = mm(base, dx[:, :TILE], NN).astype(BF16)
    act_copy.wait()


def grad_kernel(g_ref, act_ref, out_ref):
    hidden = act_ref.shape[1]
    for at in range(0, hidden, 256):
        cols = slice(at, min(at + 256, hidden))
        out_ref[:, cols] = mm(g_ref[...], act_ref[:, cols], TN).astype(BF16)


def combine_kernel(recv_ref, disp_ref, ids_ref, comb_ref, tok_ref, cot_ref, out_ref, dx_ref, grad_ref):
    rows = recv_ref.shape[0]
    feat, toks = tok_ref.shape
    half = feat // 2
    row = iota((rows, toks), 0)
    expert, main = row >> 3, row & 7 < CAP
    pick = disp_ref[:, :toks].astype(F32)
    shift = disp_ref[:, toks:].astype(F32)
    base = jnp.where(main, pick, 0.0)
    total = [tok_ref[:half, :].astype(F32), tok_ref[half:, :].astype(F32)]
    for k in range(2):
        mine = jnp.where(expert == ids_ref[k : k + 1, :], base, 0.0).astype(BF16)
        y = mm(recv_ref[:, : 2 * TILE], mine, TN)
        weight = comb_ref[k : k + 1, :]
        total = [total[i] + weight * y[TILE * i : TILE * i + half] for i in range(2)]
        grad_ref[k : k + 1, :] = (y[half : half + 1] + y[half + 1 : half + 2]) / weight
    out_ref[:half, :] = total[0].astype(BF16)
    out_ref[half:, :] = total[1].astype(BF16)
    dx_low = mm(recv_ref[:, 2 * TILE :], base.astype(BF16), TN)
    dx_high = mm(recv_ref[:, :TILE], jnp.where(main, 0.0, pick).astype(BF16), TN)
    dx_high += mm(recv_ref[:, TILE : 2 * TILE], jnp.where(main, 0.0, shift).astype(BF16), TN)
    dx_ref[:half, :] = (cot_ref[:half, :].astype(F32) + dx_low[:half]).astype(BF16)
    dx_ref[half:, :] = (cot_ref[half:, :].astype(F32) + dx_high[:half]).astype(BF16)


def exchange(rows, groups):
    parts = rows.reshape(groups, PAD, 3 * TILE)
    parts = lax.all_to_all(parts, "expert", split_axis=0, concat_axis=0, tiled=True)
    return parts.reshape(groups * PAD, 3 * TILE)


def body(tokens, cotangent, expert_ids, combine, w_up, w_down):
    toks, feat = tokens.shape
    groups = lax.axis_size("expert")
    hidden = w_up.shape[2]
    kept, padded = groups * CAP, groups * PAD
    count = kept // 16 * 2
    shape = jax.ShapeDtypeStruct
    dma = pltpu.SemaphoreType.DMA
    tok, cot, ids, comb = tokens.T, cotangent.T, expert_ids.T, combine.T
    up, down = w_up[0], w_down[0].T
    weights = [pltpu.VMEM((feat, hidden), BF16)] * 2

    send, disp = call(
        dispatch_kernel,
        (shape((padded, 3 * TILE), BF16), shape((padded, 2 * toks), BF16)),
        (VMEM, VMEM),
        (ids, comb, tok, cot),
        [HBM] * 4,
        [pltpu.VMEM(a.shape, a.dtype) for a in (ids, comb, tok, cot)] + [dma((4,))],
    )
    recv = exchange(send, groups)
    pieces = tuple(shape((16, b - a), BF16) for _ in range(kept // 16) for a, b in spans(hidden))
    g_rows, *terms = call(
        functools.partial(up_kernel, count),
        (shape((kept, feat), BF16),) + 2 * pieces,
        (VMEM,) + (HBM,) * (2 * count),
        (recv, up, down),
        [VMEM, HBM, HBM],
        [pltpu.VMEM((2, kept, hidden), BF16), *weights, dma((2,)), dma((2 * count,))],
    )
    sums = lax.psum(tuple(terms), "dp")
    send_back, act = call(
        functools.partial(down_kernel, count),
        (shape((padded, 3 * TILE), BF16), shape((kept, hidden), BF16)),
        (VMEM, HBM),
        (*sums, up, down),
        [HBM] * (2 * count + 2),
        [
            pltpu.VMEM((2, kept, hidden), BF16),
            pltpu.VMEM((kept, hidden), BF16),
            pltpu.VMEM((kept, hidden), BF16),
            pltpu.VMEM((kept, TILE), F32),
            *weights,
            dma((2 * count,)),
            dma((3,)),
        ],
    )
    back = exchange(send_back, groups)
    down_grad = call(grad_kernel, shape((feat, hidden), BF16), VMEM, (g_rows, act), [VMEM] * 2)
    layer_out, input_grad, combine_grad = call(
        combine_kernel,
        (shape((feat, toks), BF16), shape((feat, toks), BF16), shape((2, toks), F32)),
        (VMEM,) * 3,
        (back, disp, ids, comb, tok, cot),
        [VMEM] * 6,
        limit=8,
    )
    return layer_out.T, input_grad.T, combine_grad.T, down_grad.T[None]


def solution(mesh):
    in_specs = (
        P("expert", "dp"),
        P("expert", "dp"),
        P("expert", None),
        P("expert", None),
        P("expert", "dp", None),
        P("expert", None, "dp"),
    )
    out_specs = (P("expert", "dp"), P("expert", "dp"), P("expert", None), P("expert", None, "dp"))
    return jax.shard_map(body, mesh=mesh, in_specs=in_specs, out_specs=out_specs, check_vma=False)
```

```python
import functools

import jax
import jax.numpy as jnp
from jax import lax
from jax.experimental import pallas as pl
from jax.experimental.pallas import tpu as pltpu
from jax.sharding import PartitionSpec as P

CAP = 5
PAD = 8
TILE = 128
F32 = jnp.float32
BF16 = jnp.bfloat16
VMEM = pl.BlockSpec(memory_space=pltpu.VMEM)
HBM = pl.BlockSpec(memory_space=pltpu.HBM)
NN = (((1,), (0,)), ((), ()))
NT = (((1,), (1,)), ((), ()))
TN = (((0,), (0,)), ((), ()))


def mm(a, b, dims):
    return lax.dot_general(a, b, dims, preferred_element_type=F32)


def halves(block):
    half = block.shape[0] // 2
    zeros = jnp.zeros((TILE - half, block.shape[1]), block.dtype)
    return jnp.concatenate([block[:half], zeros, block[half:], zeros], axis=0)


def iota(shape, dim):
    return lax.broadcasted_iota(jnp.int32, shape, dim)


def ones_at(mask):
    return jnp.where(mask, 1.0, 0.0).astype(BF16)


def call(kernel, out_shape, out_specs, args, in_specs, scratch=(), limit=60):
    return pl.pallas_call(
        kernel,
        out_shape=out_shape,
        in_specs=in_specs,
        out_specs=out_specs,
        scratch_shapes=list(scratch),
        compiler_params=pltpu.CompilerParams(vmem_limit_bytes=limit * 1024 * 1024),
    )(*args)


def load(pairs, sems):
    copies = [pltpu.make_async_copy(src, dst, sems.at[i]) for i, (src, dst) in enumerate(pairs)]
    for copy in copies:
        copy.start()
    return copies


def ship(src_ref, dst_ref, i, sem):
    tile = slice(TILE * i, TILE * i + TILE)
    copy = pltpu.make_async_copy(src_ref.at[:, tile], dst_ref.at[:, tile], sem)
    copy.start()
    return copy


def dispatch_kernel(ids_hbm, comb_hbm, tok_hbm, cot_hbm, send_hbm, disp_hbm, *scratch):
    ids_ref, comb_ref, tok_ref, cot_ref, send_ref, disp_ref, sems, out_sems = scratch
    copies = load(((ids_hbm, ids_ref), (comb_hbm, comb_ref), (tok_hbm, tok_ref), (cot_hbm, cot_ref)), sems)
    rows, toks = send_ref.shape[0], tok_ref.shape[1]
    row = iota((rows, toks), 0)
    expert, slot = row >> 3, row & 7
    earlier = ones_at(iota((toks, toks), 0) < iota((toks, toks), 1))
    copies[0].wait()
    first = expert == ids_ref[0:1, :]
    second = expert == ids_ref[1:2, :]
    chosen = jnp.where(first | second, 1.0, 0.0)
    before = mm(chosen.astype(BF16), earlier, NN).astype(jnp.int32)
    here = [
        jnp.where(before == jnp.where(slot < CAP, slot, jnp.where(slot - shift < CAP, slot - shift, -1)), chosen, 0.0)
        for shift in (5, 2)
    ]
    copies[1].wait()
    weight = jnp.where(first, comb_ref[0:1, :], comb_ref[1:2, :])
    weights = [jnp.sum(h * weight, axis=1, keepdims=True) for h in here]
    picks = [h.astype(BF16) for h in here]
    disp_ref[:, :toks] = picks[0]
    disp_ref[:, toks:] = picks[1]
    started = [pltpu.make_async_copy(disp_ref, disp_hbm, out_sems.at[3])]
    started[0].start()
    copies[2].wait()
    copies[3].wait()
    x, g = halves(tok_ref[...]), halves(cot_ref[...])
    low = iota((rows, TILE), 0) & 7 < CAP
    for i in range(2):
        source = jnp.concatenate([x[TILE * i : TILE * i + TILE], g[TILE:]], axis=0)
        both = mm(picks[i], source, NT)
        send_ref[:, TILE * i : TILE * i + TILE] = jnp.where(low, both[:, :TILE], weights[i] * both[:, TILE:]).astype(BF16)
        started.append(ship(send_ref, send_hbm, i, out_sems.at[i]))
    send_ref[:, 2 * TILE :] = (weights[0] * mm(picks[0], g[:TILE], NT)).astype(BF16)
    started.append(ship(send_ref, send_hbm, 2, out_sems.at[2]))
    for copy in started:
        copy.wait()


def spans(hidden):
    cut = (hidden // 2 + 127) // 128 * 128
    return (0, cut), (cut, hidden)


def places(kept, hidden):
    return [(slice(r, r + 16), slice(*span)) for r in range(0, kept, 16) for span in spans(hidden)]


def up_kernel(count, recv_hbm, up_hbm, down_hbm, g_hbm, *refs):
    outs, (term_ref, recv_ref, g_ref, up_ref, down_ref, in_sems, out_sems) = refs[: 2 * count], refs[2 * count :]
    copies = load(((up_hbm, up_ref), (down_hbm, down_ref), (recv_hbm, recv_ref)), in_sems)
    feat, hidden = up_ref.shape
    half = feat // 2
    kept, padded = g_ref.shape[0], recv_ref.shape[0]
    row = iota((kept, padded), 0)
    source = (row * 13108) >> 16
    slot = row - source * CAP
    at = iota((kept, padded), 1) - source * PAD
    copies[2].wait()
    main = mm(ones_at(at == slot), recv_ref[...], NN)
    extra = mm(ones_at(at == jnp.where(slot < 3, slot + 5, padded)), recv_ref[:, :TILE], NN)
    extra += mm(ones_at(at == jnp.where(slot < 3, padded, slot + 2)), recv_ref[:, TILE : 2 * TILE], NN)
    x_rows = jnp.concatenate([main[:, :half], main[:, TILE : TILE + half]], axis=1).astype(BF16)
    g_rows = jnp.concatenate([main[:, 2 * TILE : 2 * TILE + half], extra[:, :half]], axis=1).astype(BF16)
    g_ref[...] = g_rows
    started = [pltpu.make_async_copy(g_ref, g_hbm, out_sems.at[2 * count])]
    started[0].start()
    for k, (rows, w_ref) in enumerate(((x_rows, up_ref), (g_rows, down_ref))):
        copies[k].wait()
        for at in range(0, hidden, 256):
            cols = slice(at, min(at + 256, hidden))
            term_ref[k, :, cols] = mm(rows, w_ref[:, cols], NN).astype(BF16)
        for i, (r, c) in enumerate(places(kept, hidden), k * count):
            copy = pltpu.make_async_copy(term_ref.at[k, r, c], outs[i], out_sems.at[i])
            copy.start()
            started.append(copy)
    for copy in started:
        copy.wait()


def down_kernel(count, *refs):
    sums, (up_hbm, down_hbm) = refs[: 2 * count], refs[2 * count : 2 * count + 2]
    send_hbm, act_hbm, sum_ref, act_ref, dhid_ref, dots_ref, up_ref, down_ref, send_ref, sems, w_sems = refs[2 * count + 2 :]
    kept, hidden = act_ref.shape
    padded, feat = send_ref.shape[0], up_ref.shape[0]
    half = feat // 2
    waits = {}
    for i, (r, c) in enumerate(places(kept, hidden)):
        for k in range(2):
            copy = pltpu.make_async_copy(sums[k * count + i], sum_ref.at[k, r, c], sems.at[k * count + i])
            copy.start()
            waits.setdefault(r.start, []).append(copy)
    copies = load(((up_hbm, up_ref), (down_hbm, down_ref)), w_sems)
    for first in range(0, kept, 16):
        for copy in waits[first]:
            copy.wait()
        rows = slice(first, first + 16)
        h = sum_ref[0, rows, :].astype(F32)
        d = sum_ref[1, rows, :].astype(F32)
        s = 1.0 / (1.0 + jnp.exp(-h))
        act = (h * s).astype(BF16)
        act_ref[rows, :] = act
        dhid_ref[rows, :] = (d * (s * (1.0 + h * (1.0 - s)))).astype(BF16)
        dots_ref[rows, :] = jnp.broadcast_to(jnp.sum(act.astype(F32) * d, axis=1, keepdims=True), (16, TILE))
    act_copy = pltpu.make_async_copy(act_ref, act_hbm, w_sems.at[2])
    act_copy.start()
    row = iota((padded, kept), 0)
    slot = row & 7
    at = iota((padded, kept), 1) - (row >> 3) * CAP
    base = ones_at((at == slot) & (slot < CAP))
    copies[1].wait()
    y = mm(act_ref[...], halves(down_ref[...]), NT).astype(BF16)
    dots = dots_ref[...]
    high = dots.astype(BF16).astype(F32)
    lane = iota((kept, TILE), 1)
    low = jnp.where(lane == half, high, jnp.where(lane == half + 1, dots - high, y[:, :TILE].astype(F32))).astype(BF16)
    copies[0].wait()
    dx = mm(dhid_ref[...], halves(up_ref[...]), NT).astype(BF16)
    send_ref[:, 2 * TILE :] = mm(base, dx[:, :TILE], NN).astype(BF16)
    started = [act_copy, ship(send_ref, send_hbm, 2, w_sems.at[5])]
    for i, (part, shift) in enumerate(((low, 5), (y[:, TILE:], 2))):
        lift = ones_at((slot >= CAP) & (slot - shift < (3 if i == 0 else CAP)) & (at == slot - shift))
        tile = mm(base, part, NN) + mm(lift, dx[:, TILE:], NN)
        send_ref[:, TILE * i : TILE * i + TILE] = tile.astype(BF16)
        started.append(ship(send_ref, send_hbm, i, w_sems.at[3 + i]))
    for copy in started:
        copy.wait()


def grad_kernel(g_ref, act_ref, out_ref):
    hidden = act_ref.shape[1]
    for at in range(0, hidden, 256):
        cols = slice(at, min(at + 256, hidden))
        out_ref[:, cols] = mm(g_ref[...], act_ref[:, cols], TN).astype(BF16)


def combine_kernel(recv_ref, disp_ref, ids_ref, comb_ref, tok_ref, cot_ref, out_ref, dx_ref, grad_ref):
    rows = recv_ref.shape[0]
    feat, toks = tok_ref.shape
    half = feat // 2
    row = iota((rows, toks), 0)
    expert, main = row >> 3, row & 7 < CAP
    pick = disp_ref[:, :toks].astype(F32)
    shift = disp_ref[:, toks:].astype(F32)
    base = jnp.where(main, pick, 0.0)
    total = [tok_ref[:half, :].astype(F32), tok_ref[half:, :].astype(F32)]
    for k in range(2):
        mine = jnp.where(expert == ids_ref[k : k + 1, :], base, 0.0).astype(BF16)
        y = mm(recv_ref[:, : 2 * TILE], mine, TN)
        weight = comb_ref[k : k + 1, :]
        total = [total[i] + weight * y[TILE * i : TILE * i + half] for i in range(2)]
        grad_ref[k : k + 1, :] = (y[half : half + 1] + y[half + 1 : half + 2]) / weight
    out_ref[:half, :] = total[0].astype(BF16)
    out_ref[half:, :] = total[1].astype(BF16)
    dx_low = mm(recv_ref[:, 2 * TILE :], base.astype(BF16), TN)
    dx_high = mm(recv_ref[:, :TILE], jnp.where(main, 0.0, pick).astype(BF16), TN)
    dx_high += mm(recv_ref[:, TILE : 2 * TILE], jnp.where(main, 0.0, shift).astype(BF16), TN)
    dx_ref[:half, :] = (cot_ref[:half, :].astype(F32) + dx_low[:half]).astype(BF16)
    dx_ref[half:, :] = (cot_ref[half:, :].astype(F32) + dx_high[:half]).astype(BF16)


def exchange(rows, groups):
    parts = rows.reshape(groups, PAD, 3 * TILE)
    parts = lax.all_to_all(parts, "expert", split_axis=0, concat_axis=0, tiled=True)
    return parts.reshape(groups * PAD, 3 * TILE)


def body(tokens, cotangent, expert_ids, combine, w_up, w_down):
    toks, feat = tokens.shape
    groups = lax.axis_size("expert")
    hidden = w_up.shape[2]
    kept, padded = groups * CAP, groups * PAD
    shape = jax.ShapeDtypeStruct
    dma = pltpu.SemaphoreType.DMA
    tok, cot, ids, comb = tokens.T, cotangent.T, expert_ids.T, combine.T
    up, down = w_up[0], w_down[0].T
    weights = [pltpu.VMEM((feat, hidden), BF16)] * 2

    send, disp = call(
        dispatch_kernel,
        (shape((padded, 3 * TILE), BF16), shape((padded, 2 * toks), BF16)),
        (HBM, HBM),
        (ids, comb, tok, cot),
        [HBM] * 4,
        [pltpu.VMEM(a.shape, a.dtype) for a in (ids, comb, tok, cot)]
        + [pltpu.VMEM((padded, 3 * TILE), BF16), pltpu.VMEM((padded, 2 * toks), BF16), dma((4,)), dma((4,))],
    )
    recv = exchange(send, groups)
    pieces = tuple(shape((r.stop - r.start, c.stop - c.start), BF16) for r, c in places(kept, hidden))
    count = len(pieces)
    g_rows, *terms = call(
        functools.partial(up_kernel, count),
        (shape((kept, feat), BF16),) + 2 * pieces,
        (HBM,) * (1 + 2 * count),
        (recv, up, down),
        [HBM] * 3,
        [
            pltpu.VMEM((2, kept, hidden), BF16),
            pltpu.VMEM((padded, 3 * TILE), BF16),
            pltpu.VMEM((kept, feat), BF16),
            *weights,
            dma((3,)),
            dma((2 * count + 1,)),
        ],
    )
    sums = lax.psum(tuple(terms), "dp")
    send_back, act = call(
        functools.partial(down_kernel, count),
        (shape((padded, 3 * TILE), BF16), shape((kept, hidden), BF16)),
        (HBM, HBM),
        (*sums, up, down),
        [HBM] * (2 * count + 2),
        [
            pltpu.VMEM((2, kept, hidden), BF16),
            pltpu.VMEM((kept, hidden), BF16),
            pltpu.VMEM((kept, hidden), BF16),
            pltpu.VMEM((kept, TILE), F32),
            *weights,
            pltpu.VMEM((padded, 3 * TILE), BF16),
            dma((2 * count,)),
            dma((6,)),
        ],
    )
    back = exchange(send_back, groups)
    down_grad = call(grad_kernel, shape((feat, hidden), BF16), VMEM, (g_rows, act), [VMEM] * 2)
    layer_out, input_grad, combine_grad = call(
        combine_kernel,
        (shape((feat, toks), BF16), shape((feat, toks), BF16), shape((2, toks), F32)),
        (VMEM,) * 3,
        (back, disp, ids, comb, tok, cot),
        [VMEM] * 6,
        limit=8,
    )
    return layer_out.T, input_grad.T, combine_grad.T, down_grad.T[None]


def solution(mesh):
    in_specs = (
        P("expert", "dp"),
        P("expert", "dp"),
        P("expert", None),
        P("expert", None),
        P("expert", "dp", None),
        P("expert", None, "dp"),
    )
    out_specs = (P("expert", "dp"), P("expert", "dp"), P("expert", None), P("expert", None, "dp"))
    return jax.shard_map(body, mesh=mesh, in_specs=in_specs, out_specs=out_specs, check_vma=False)
```

```python
import functools

import jax
import jax.numpy as jnp
from jax import lax
from jax.experimental import pallas as pl
from jax.experimental.pallas import tpu as pltpu
from jax.sharding import PartitionSpec as P

CAP = 5
PAD = 8
TILE = 128
F32 = jnp.float32
BF16 = jnp.bfloat16
VMEM = pl.BlockSpec(memory_space=pltpu.VMEM)
HBM = pl.BlockSpec(memory_space=pltpu.HBM)
NN = (((1,), (0,)), ((), ()))
NT = (((1,), (1,)), ((), ()))
TN = (((0,), (0,)), ((), ()))


def mm(a, b, dims):
    return lax.dot_general(a, b, dims, preferred_element_type=F32)


def halves(block):
    half = block.shape[0] // 2
    zeros = jnp.zeros((TILE - half, block.shape[1]), block.dtype)
    return jnp.concatenate([block[:half], zeros, block[half:], zeros], axis=0)


def iota(shape, dim):
    return lax.broadcasted_iota(jnp.int32, shape, dim)


def ones_at(mask):
    return jnp.where(mask, 1.0, 0.0).astype(BF16)


def call(kernel, out_shape, out_specs, args, in_specs, scratch=(), limit=60):
    return pl.pallas_call(
        kernel,
        out_shape=out_shape,
        in_specs=in_specs,
        out_specs=out_specs,
        scratch_shapes=list(scratch),
        compiler_params=pltpu.CompilerParams(vmem_limit_bytes=limit * 1024 * 1024),
    )(*args)


def load(pairs, sems):
    copies = [pltpu.make_async_copy(src, dst, sems.at[i]) for i, (src, dst) in enumerate(pairs)]
    for copy in copies:
        copy.start()
    return copies


def ship(src_ref, dst_ref, i, sem):
    tile = slice(TILE * i, TILE * i + TILE)
    copy = pltpu.make_async_copy(src_ref.at[:, tile], dst_ref.at[:, tile], sem)
    copy.start()
    return copy


def dispatch_kernel(ids_hbm, comb_hbm, tok_hbm, cot_hbm, send_hbm, disp_hbm, *scratch):
    ids_ref, comb_ref, tok_ref, cot_ref, send_ref, disp_ref, sems, out_sems = scratch
    copies = load(((ids_hbm, ids_ref), (comb_hbm, comb_ref), (tok_hbm, tok_ref), (cot_hbm, cot_ref)), sems)
    rows, toks = send_ref.shape[0], tok_ref.shape[1]
    row = iota((rows, toks), 0)
    expert, slot = row >> 3, row & 7
    earlier = ones_at(iota((toks, toks), 0) < iota((toks, toks), 1))
    copies[0].wait()
    first = expert == ids_ref[0:1, :]
    second = expert == ids_ref[1:2, :]
    chosen = jnp.where(first | second, 1.0, 0.0)
    before = mm(chosen.astype(BF16), earlier, NN).astype(jnp.int32)
    here = [
        jnp.where(before == jnp.where(slot < CAP, slot, jnp.where(slot - shift < CAP, slot - shift, -1)), chosen, 0.0)
        for shift in (5, 2)
    ]
    copies[1].wait()
    weight = jnp.where(first, comb_ref[0:1, :], comb_ref[1:2, :])
    weights = [jnp.sum(h * weight, axis=1, keepdims=True) for h in here]
    picks = [h.astype(BF16) for h in here]
    disp_ref[:, :toks] = picks[0]
    disp_ref[:, toks:] = picks[1]
    started = [pltpu.make_async_copy(disp_ref, disp_hbm, out_sems.at[3])]
    started[0].start()
    copies[2].wait()
    copies[3].wait()
    x, g = halves(tok_ref[...]), halves(cot_ref[...])
    low = iota((rows, TILE), 0) & 7 < CAP
    for i in range(2):
        source = jnp.concatenate([x[TILE * i : TILE * i + TILE], g[TILE:]], axis=0)
        both = mm(picks[i], source, NT)
        send_ref[:, TILE * i : TILE * i + TILE] = jnp.where(low, both[:, :TILE], weights[i] * both[:, TILE:]).astype(BF16)
        started.append(ship(send_ref, send_hbm, i, out_sems.at[i]))
    send_ref[:, 2 * TILE :] = (weights[0] * mm(picks[0], g[:TILE], NT)).astype(BF16)
    started.append(ship(send_ref, send_hbm, 2, out_sems.at[2]))
    for copy in started:
        copy.wait()


def chunks(hidden):
    return [slice(at, min(at + 256, hidden)) for at in range(0, hidden, 256)]


def places(kept, hidden):
    return [(slice(r, r + 80), c) for c in chunks(hidden) for r in range(0, kept, 80)]


def up_kernel(count, recv_hbm, up_hbm, down_hbm, g_hbm, *refs):
    outs, (term_ref, recv_ref, g_ref, up_ref, down_ref, in_sems, out_sems) = refs[: 2 * count], refs[2 * count :]
    copies = load(((up_hbm, up_ref), (down_hbm, down_ref), (recv_hbm, recv_ref)), in_sems)
    feat, hidden = up_ref.shape
    half = feat // 2
    kept, padded = g_ref.shape[0], recv_ref.shape[0]
    row = iota((kept, padded), 0)
    source = (row * 13108) >> 16
    slot = row - source * CAP
    at = iota((kept, padded), 1) - source * PAD
    copies[2].wait()
    main = mm(ones_at(at == slot), recv_ref[...], NN)
    extra = mm(ones_at(at == jnp.where(slot < 3, slot + 5, padded)), recv_ref[:, :TILE], NN)
    extra += mm(ones_at(at == jnp.where(slot < 3, padded, slot + 2)), recv_ref[:, TILE : 2 * TILE], NN)
    x_rows = jnp.concatenate([main[:, :half], main[:, TILE : TILE + half]], axis=1).astype(BF16)
    g_rows = jnp.concatenate([main[:, 2 * TILE : 2 * TILE + half], extra[:, :half]], axis=1).astype(BF16)
    g_ref[...] = g_rows
    started = [pltpu.make_async_copy(g_ref, g_hbm, out_sems.at[2 * count])]
    started[0].start()
    where = places(kept, hidden)
    for k, (rows, w_ref) in enumerate(((x_rows, up_ref), (g_rows, down_ref))):
        copies[k].wait()
        for cols in chunks(hidden):
            term_ref[k, :, cols] = mm(rows, w_ref[:, cols], NN).astype(BF16)
            for i, (r, c) in enumerate(where, k * count):
                if c == cols:
                    copy = pltpu.make_async_copy(term_ref.at[k, r, c], outs[i], out_sems.at[i])
                    copy.start()
                    started.append(copy)
    for copy in started:
        copy.wait()


def down_kernel(count, *refs):
    sums, (up_hbm, down_hbm) = refs[: 2 * count], refs[2 * count : 2 * count + 2]
    send_hbm, act_hbm, sum_ref, act_ref, dhid_ref, dots_ref, y_ref, dx_ref, up_ref, down_ref, send_ref, sems, w_sems = refs[
        2 * count + 2 :
    ]
    kept, hidden = act_ref.shape
    padded, half = send_ref.shape[0], up_hbm.shape[0] // 2
    where = places(kept, hidden)
    parts = chunks(hidden)

    def fetch(cols):
        copies = []
        for i, (r, c) in enumerate(where):
            if c == cols:
                for k in range(2):
                    copy = pltpu.make_async_copy(sums[k * count + i], sum_ref.at[k, r, c], sems.at[k * count + i])
                    copy.start()
                    copies.append(copy)
        return copies

    waits = [fetch(parts[0])]
    halved = [
        (src.at[slice(half * i, half * i + half), :], dst.at[slice(TILE * i, TILE * i + half), :])
        for src, dst in ((up_hbm, up_ref), (down_hbm, down_ref))
        for i in range(2)
    ]
    copies = load(halved, w_sems)
    waits += [fetch(cols) for cols in parts[1:]]
    for ref in (up_ref, down_ref):
        for i in range(2):
            ref[TILE * i + half : TILE * i + TILE, :] = jnp.zeros((TILE - half, hidden), BF16)

    def products(cols, first):
        y = mm(act_ref[:, cols], down_ref[:, cols], NT)
        dx = mm(dhid_ref[:, cols], up_ref[:, cols], NT)
        y_ref[...] = y if first else y_ref[...] + y
        dx_ref[...] = dx if first else dx_ref[...] + dx

    started = []
    for n, cols in enumerate(parts):
        if n == 0:
            for copy in sum(waits, []) + copies:
                copy.wait()
        for at in range(0, kept, 16):
            rows = slice(at, at + 16)
            h = sum_ref[0, rows, cols].astype(F32)
            d = sum_ref[1, rows, cols].astype(F32)
            s = 1.0 / (1.0 + jnp.exp(-h))
            act = (h * s).astype(BF16)
            act_ref[rows, cols] = act
            dhid_ref[rows, cols] = (d * (s * (1.0 + h * (1.0 - s)))).astype(BF16)
            dot = act.astype(F32) * d
            dot = sum(dot[:, lane : lane + TILE] for lane in range(0, dot.shape[1], TILE))
            dots_ref[rows, :] = dot if n == 0 else dots_ref[rows, :] + dot
        if n > 0:
            products(parts[n - 1], n == 1)
    started.append(pltpu.make_async_copy(act_ref, act_hbm, w_sems.at[4]))
    started[0].start()
    products(parts[-1], len(parts) == 1)
    row = iota((padded, kept), 0)
    slot = row & 7
    at = iota((padded, kept), 1) - (row >> 3) * CAP
    base = ones_at((at == slot) & (slot < CAP))
    y, dx = y_ref[...].astype(BF16), dx_ref[...].astype(BF16)
    dots = jnp.sum(dots_ref[...], axis=1, keepdims=True)
    high = dots.astype(BF16).astype(F32)
    lane = iota((kept, TILE), 1)
    low = jnp.where(lane == half, high, jnp.where(lane == half + 1, dots - high, y[:, :TILE].astype(F32))).astype(BF16)
    send_ref[:, 2 * TILE :] = mm(base, dx[:, :TILE], NN).astype(BF16)
    started.append(ship(send_ref, send_hbm, 2, w_sems.at[7]))
    for i, (part, shift) in enumerate(((low, 5), (y[:, TILE:], 2))):
        lift = ones_at((slot >= CAP) & (slot - shift < (3 if i == 0 else CAP)) & (at == slot - shift))
        tile = mm(base, part, NN) + mm(lift, dx[:, TILE:], NN)
        send_ref[:, TILE * i : TILE * i + TILE] = tile.astype(BF16)
        started.append(ship(send_ref, send_hbm, i, w_sems.at[5 + i]))
    for copy in started:
        copy.wait()


def grad_kernel(g_ref, act_ref, out_ref):
    hidden = act_ref.shape[1]
    for at in range(0, hidden, 256):
        cols = slice(at, min(at + 256, hidden))
        out_ref[:, cols] = mm(g_ref[...], act_ref[:, cols], TN).astype(BF16)


def combine_kernel(recv_ref, disp_ref, ids_ref, comb_ref, tok_ref, cot_ref, out_ref, dx_ref, grad_ref):
    rows = recv_ref.shape[0]
    feat, toks = tok_ref.shape
    half = feat // 2
    row = iota((rows, toks), 0)
    expert, main = row >> 3, row & 7 < CAP
    pick = disp_ref[:, :toks].astype(F32)
    shift = disp_ref[:, toks:].astype(F32)
    base = jnp.where(main, pick, 0.0)
    total = [tok_ref[:half, :].astype(F32), tok_ref[half:, :].astype(F32)]
    for k in range(2):
        mine = jnp.where(expert == ids_ref[k : k + 1, :], base, 0.0).astype(BF16)
        y = mm(recv_ref[:, : 2 * TILE], mine, TN)
        weight = comb_ref[k : k + 1, :]
        total = [total[i] + weight * y[TILE * i : TILE * i + half] for i in range(2)]
        grad_ref[k : k + 1, :] = (y[half : half + 1] + y[half + 1 : half + 2]) / weight
    out_ref[:half, :] = total[0].astype(BF16)
    out_ref[half:, :] = total[1].astype(BF16)
    dx_low = mm(recv_ref[:, 2 * TILE :], base.astype(BF16), TN)
    dx_high = mm(recv_ref[:, :TILE], jnp.where(main, 0.0, pick).astype(BF16), TN)
    dx_high += mm(recv_ref[:, TILE : 2 * TILE], jnp.where(main, 0.0, shift).astype(BF16), TN)
    dx_ref[:half, :] = (cot_ref[:half, :].astype(F32) + dx_low[:half]).astype(BF16)
    dx_ref[half:, :] = (cot_ref[half:, :].astype(F32) + dx_high[:half]).astype(BF16)


def exchange(rows, groups):
    parts = rows.reshape(groups, PAD, 3 * TILE)
    parts = lax.all_to_all(parts, "expert", split_axis=0, concat_axis=0, tiled=True)
    return parts.reshape(groups * PAD, 3 * TILE)


def body(tokens, cotangent, expert_ids, combine, w_up, w_down):
    toks, feat = tokens.shape
    groups = lax.axis_size("expert")
    hidden = w_up.shape[2]
    kept, padded = groups * CAP, groups * PAD
    shape = jax.ShapeDtypeStruct
    dma = pltpu.SemaphoreType.DMA
    tok, cot, ids, comb = tokens.T, cotangent.T, expert_ids.T, combine.T
    up, down = w_up[0], w_down[0].T
    weights = [pltpu.VMEM((feat, hidden), BF16)] * 2

    send, disp = call(
        dispatch_kernel,
        (shape((padded, 3 * TILE), BF16), shape((padded, 2 * toks), BF16)),
        (HBM, HBM),
        (ids, comb, tok, cot),
        [HBM] * 4,
        [pltpu.VMEM(a.shape, a.dtype) for a in (ids, comb, tok, cot)]
        + [pltpu.VMEM((padded, 3 * TILE), BF16), pltpu.VMEM((padded, 2 * toks), BF16), dma((4,)), dma((4,))],
    )
    recv = exchange(send, groups)
    pieces = tuple(shape((r.stop - r.start, c.stop - c.start), BF16) for r, c in places(kept, hidden))
    count = len(pieces)
    g_rows, *terms = call(
        functools.partial(up_kernel, count),
        (shape((kept, feat), BF16),) + 2 * pieces,
        (HBM,) * (1 + 2 * count),
        (recv, up, down),
        [HBM] * 3,
        [
            pltpu.VMEM((2, kept, hidden), BF16),
            pltpu.VMEM((padded, 3 * TILE), BF16),
            pltpu.VMEM((kept, feat), BF16),
            *weights,
            dma((3,)),
            dma((2 * count + 1,)),
        ],
    )
    sums = lax.psum(tuple(terms), "dp")
    send_back, act = call(
        functools.partial(down_kernel, count),
        (shape((padded, 3 * TILE), BF16), shape((kept, hidden), BF16)),
        (HBM, HBM),
        (*sums, up, down),
        [HBM] * (2 * count + 2),
        [
            pltpu.VMEM((2, kept, hidden), BF16),
            pltpu.VMEM((kept, hidden), BF16),
            pltpu.VMEM((kept, hidden), BF16),
            pltpu.VMEM((kept, TILE), F32),
            pltpu.VMEM((kept, 2 * TILE), F32),
            pltpu.VMEM((kept, 2 * TILE), F32),
            pltpu.VMEM((2 * TILE, hidden), BF16),
            pltpu.VMEM((2 * TILE, hidden), BF16),
            pltpu.VMEM((padded, 3 * TILE), BF16),
            dma((2 * count,)),
            dma((8,)),
        ],
    )
    back = exchange(send_back, groups)
    down_grad = call(grad_kernel, shape((feat, hidden), BF16), VMEM, (g_rows, act), [VMEM] * 2)
    layer_out, input_grad, combine_grad = call(
        combine_kernel,
        (shape((feat, toks), BF16), shape((feat, toks), BF16), shape((2, toks), F32)),
        (VMEM,) * 3,
        (back, disp, ids, comb, tok, cot),
        [VMEM] * 6,
        limit=8,
    )
    return layer_out.T, input_grad.T, combine_grad.T, down_grad.T[None]


def solution(mesh):
    in_specs = (
        P("expert", "dp"),
        P("expert", "dp"),
        P("expert", None),
        P("expert", None),
        P("expert", "dp", None),
        P("expert", None, "dp"),
    )
    out_specs = (P("expert", "dp"), P("expert", "dp"), P("expert", None), P("expert", None, "dp"))
    return jax.shard_map(body, mesh=mesh, in_specs=in_specs, out_specs=out_specs, check_vma=False)
```

```python
import functools

import jax
import jax.numpy as jnp
from jax import lax
from jax.experimental import pallas as pl
from jax.experimental.pallas import tpu as pltpu
from jax.sharding import PartitionSpec as P

CAP = 5
PAD = 8
TILE = 128
F32 = jnp.float32
BF16 = jnp.bfloat16
VMEM = pl.BlockSpec(memory_space=pltpu.VMEM)
HBM = pl.BlockSpec(memory_space=pltpu.HBM)
NN = (((1,), (0,)), ((), ()))
NT = (((1,), (1,)), ((), ()))
TN = (((0,), (0,)), ((), ()))


def mm(a, b, dims):
    return lax.dot_general(a, b, dims, preferred_element_type=F32)


def halves(block):
    half = block.shape[0] // 2
    zeros = jnp.zeros((TILE - half, block.shape[1]), block.dtype)
    return jnp.concatenate([block[:half], zeros, block[half:], zeros], axis=0)


def iota(shape, dim):
    return lax.broadcasted_iota(jnp.int32, shape, dim)


def ones_at(mask):
    return jnp.where(mask, 1.0, 0.0).astype(BF16)


def call(kernel, out_shape, out_specs, args, in_specs, scratch=(), limit=60):
    return pl.pallas_call(
        kernel,
        out_shape=out_shape,
        in_specs=in_specs,
        out_specs=out_specs,
        scratch_shapes=list(scratch),
        compiler_params=pltpu.CompilerParams(vmem_limit_bytes=limit * 1024 * 1024),
    )(*args)


def load(pairs, sems):
    copies = [pltpu.make_async_copy(src, dst, sems.at[i]) for i, (src, dst) in enumerate(pairs)]
    for copy in copies:
        copy.start()
    return copies


def ship(src_ref, dst_ref, i, sem):
    tile = slice(TILE * i, TILE * i + TILE)
    copy = pltpu.make_async_copy(src_ref.at[:, tile], dst_ref.at[:, tile], sem)
    copy.start()
    return copy


def dispatch_kernel(ids_hbm, comb_hbm, tok_hbm, cot_hbm, send_hbm, disp_hbm, *scratch):
    ids_ref, comb_ref, tok_ref, cot_ref, send_ref, disp_ref, sems, out_sems = scratch
    copies = load(((ids_hbm, ids_ref), (comb_hbm, comb_ref), (tok_hbm, tok_ref), (cot_hbm, cot_ref)), sems)
    rows, toks = send_ref.shape[0], tok_ref.shape[1]
    row = iota((rows, toks), 0)
    expert, slot = row >> 3, row & 7
    earlier = ones_at(iota((toks, toks), 0) < iota((toks, toks), 1))
    copies[0].wait()
    first = expert == ids_ref[0:1, :]
    second = expert == ids_ref[1:2, :]
    chosen = jnp.where(first | second, 1.0, 0.0)
    before = mm(chosen.astype(BF16), earlier, NN).astype(jnp.int32)
    here = [
        jnp.where(before == jnp.where(slot < CAP, slot, jnp.where(slot - shift < CAP, slot - shift, -1)), chosen, 0.0)
        for shift in (5, 2)
    ]
    copies[1].wait()
    weight = jnp.where(first, comb_ref[0:1, :], comb_ref[1:2, :])
    weights = [jnp.sum(h * weight, axis=1, keepdims=True) for h in here]
    picks = [h.astype(BF16) for h in here]
    disp_ref[:, :toks] = picks[0]
    disp_ref[:, toks:] = picks[1]
    started = [pltpu.make_async_copy(disp_ref, disp_hbm, out_sems.at[3])]
    started[0].start()
    copies[2].wait()
    copies[3].wait()
    x, g = halves(tok_ref[...]), halves(cot_ref[...])
    low = iota((rows, TILE), 0) & 7 < CAP
    for i in range(2):
        source = jnp.concatenate([x[TILE * i : TILE * i + TILE], g[TILE:]], axis=0)
        both = mm(picks[i], source, NT)
        send_ref[:, TILE * i : TILE * i + TILE] = jnp.where(low, both[:, :TILE], weights[i] * both[:, TILE:]).astype(BF16)
        started.append(ship(send_ref, send_hbm, i, out_sems.at[i]))
    send_ref[:, 2 * TILE :] = (weights[0] * mm(picks[0], g[:TILE], NT)).astype(BF16)
    started.append(ship(send_ref, send_hbm, 2, out_sems.at[2]))
    for copy in started:
        copy.wait()


def chunks(hidden):
    return [slice(at, min(at + 256, hidden)) for at in range(0, hidden, 256)]


def places(kept, hidden):
    return [(slice(r, r + 80), c) for c in chunks(hidden) for r in range(0, kept, 80)]


def up_kernel(count, recv_hbm, up_hbm, down_hbm, g_hbm, *refs):
    outs, (term_ref, recv_ref, g_ref, up_ref, down_ref, in_sems, out_sems) = refs[: 2 * count], refs[2 * count :]
    copies = load(((recv_hbm, recv_ref), (up_hbm, up_ref), (down_hbm, down_ref)), in_sems)
    feat, hidden = up_ref.shape
    half = feat // 2
    kept, padded = g_ref.shape[0], recv_ref.shape[0]
    row = iota((kept, padded), 0)
    source = (row * 13108) >> 16
    slot = row - source * CAP
    at = iota((kept, padded), 1) - source * PAD
    copies[0].wait()
    main = mm(ones_at(at == slot), recv_ref[...], NN)
    extra = mm(ones_at(at == jnp.where(slot < 3, slot + 5, padded)), recv_ref[:, :TILE], NN)
    extra += mm(ones_at(at == jnp.where(slot < 3, padded, slot + 2)), recv_ref[:, TILE : 2 * TILE], NN)
    x_rows = jnp.concatenate([main[:, :half], main[:, TILE : TILE + half]], axis=1).astype(BF16)
    g_rows = jnp.concatenate([main[:, 2 * TILE : 2 * TILE + half], extra[:, :half]], axis=1).astype(BF16)
    g_ref[...] = g_rows
    started = [pltpu.make_async_copy(g_ref, g_hbm, out_sems.at[2 * count])]
    started[0].start()
    copies[1].wait()
    copies[2].wait()
    where = places(kept, hidden)
    for k, (rows, w_ref) in enumerate(((x_rows, up_ref), (g_rows, down_ref))):
        for cols in chunks(hidden):
            term_ref[k, :, cols] = mm(rows, w_ref[:, cols], NN).astype(BF16)
            for i, (r, c) in enumerate(where, k * count):
                if c == cols:
                    copy = pltpu.make_async_copy(term_ref.at[k, r, c], outs[i], out_sems.at[i])
                    copy.start()
                    started.append(copy)
    for copy in started:
        copy.wait()


def down_kernel(count, *refs):
    sums, (up_hbm, down_hbm) = refs[: 2 * count], refs[2 * count : 2 * count + 2]
    send_hbm, act_hbm, sum_ref, act_ref, dhid_ref, dots_ref, y_ref, dx_ref, up_ref, down_ref, send_ref, sems, w_sems = refs[
        2 * count + 2 :
    ]
    kept, hidden = act_ref.shape
    padded, half = send_ref.shape[0], up_hbm.shape[0] // 2
    where = places(kept, hidden)
    parts = chunks(hidden)

    def fetch(cols):
        copies = []
        for i, (r, c) in enumerate(where):
            if c == cols:
                for k in range(2):
                    copy = pltpu.make_async_copy(sums[k * count + i], sum_ref.at[k, r, c], sems.at[k * count + i])
                    copy.start()
                    copies.append(copy)
        return copies

    waits = [fetch(parts[0])]
    halved = [
        (src.at[slice(half * i, half * i + half), :], dst.at[slice(TILE * i, TILE * i + half), :])
        for src, dst in ((up_hbm, up_ref), (down_hbm, down_ref))
        for i in range(2)
    ]
    copies = load(halved, w_sems)
    waits += [fetch(cols) for cols in parts[1:]]
    for ref in (up_ref, down_ref):
        for i in range(2):
            ref[TILE * i + half : TILE * i + TILE, :] = jnp.zeros((TILE - half, hidden), BF16)

    def products(cols, first):
        y = mm(act_ref[:, cols], down_ref[:, cols], NT)
        dx = mm(dhid_ref[:, cols], up_ref[:, cols], NT)
        y_ref[...] = y if first else y_ref[...] + y
        dx_ref[...] = dx if first else dx_ref[...] + dx

    started = []
    for n, cols in enumerate(parts):
        if n == 0:
            for copy in sum(waits, []) + copies:
                copy.wait()
        for at in range(0, kept, 16):
            rows = slice(at, at + 16)
            h = sum_ref[0, rows, cols].astype(F32)
            d = sum_ref[1, rows, cols].astype(F32)
            s = 1.0 / (1.0 + jnp.exp(-h))
            act = (h * s).astype(BF16)
            act_ref[rows, cols] = act
            dhid_ref[rows, cols] = (d * (s * (1.0 + h * (1.0 - s)))).astype(BF16)
            dot = act.astype(F32) * d
            dot = sum(dot[:, lane : lane + TILE] for lane in range(0, dot.shape[1], TILE))
            dots_ref[rows, :] = dot if n == 0 else dots_ref[rows, :] + dot
        if n > 0:
            products(parts[n - 1], n == 1)
    started.append(pltpu.make_async_copy(act_ref, act_hbm, w_sems.at[4]))
    started[0].start()
    products(parts[-1], len(parts) == 1)
    row = iota((padded, kept), 0)
    slot = row & 7
    at = iota((padded, kept), 1) - (row >> 3) * CAP
    base = ones_at((at == slot) & (slot < CAP))
    y, dx = y_ref[...].astype(BF16), dx_ref[...].astype(BF16)
    dots = jnp.sum(dots_ref[...], axis=1, keepdims=True)
    high = dots.astype(BF16).astype(F32)
    lane = iota((kept, TILE), 1)
    low = jnp.where(lane == half, high, jnp.where(lane == half + 1, dots - high, y[:, :TILE].astype(F32))).astype(BF16)
    send_ref[:, 2 * TILE :] = mm(base, dx[:, :TILE], NN).astype(BF16)
    started.append(ship(send_ref, send_hbm, 2, w_sems.at[7]))
    for i, (part, shift) in enumerate(((low, 5), (y[:, TILE:], 2))):
        lift = ones_at((slot >= CAP) & (slot - shift < (3 if i == 0 else CAP)) & (at == slot - shift))
        tile = mm(base, part, NN) + mm(lift, dx[:, TILE:], NN)
        send_ref[:, TILE * i : TILE * i + TILE] = tile.astype(BF16)
        started.append(ship(send_ref, send_hbm, i, w_sems.at[5 + i]))
    for copy in started:
        copy.wait()


def grad_kernel(g_ref, act_ref, out_ref):
    hidden = act_ref.shape[1]
    for at in range(0, hidden, 256):
        cols = slice(at, min(at + 256, hidden))
        out_ref[:, cols] = mm(g_ref[...], act_ref[:, cols], TN).astype(BF16)


def combine_kernel(recv_ref, disp_ref, ids_ref, comb_ref, tok_ref, cot_ref, out_ref, dx_ref, grad_ref):
    rows = recv_ref.shape[0]
    feat, toks = tok_ref.shape
    half = feat // 2
    row = iota((rows, toks), 0)
    expert, main = row >> 3, row & 7 < CAP
    pick = disp_ref[:, :toks].astype(F32)
    shift = disp_ref[:, toks:].astype(F32)
    base = jnp.where(main, pick, 0.0)
    total = [tok_ref[:half, :].astype(F32), tok_ref[half:, :].astype(F32)]
    for k in range(2):
        mine = jnp.where(expert == ids_ref[k : k + 1, :], base, 0.0).astype(BF16)
        y = mm(recv_ref[:, : 2 * TILE], mine, TN)
        weight = comb_ref[k : k + 1, :]
        total = [total[i] + weight * y[TILE * i : TILE * i + half] for i in range(2)]
        grad_ref[k : k + 1, :] = (y[half : half + 1] + y[half + 1 : half + 2]) / weight
    out_ref[:half, :] = total[0].astype(BF16)
    out_ref[half:, :] = total[1].astype(BF16)
    dx_low = mm(recv_ref[:, 2 * TILE :], base.astype(BF16), TN)
    dx_high = mm(recv_ref[:, :TILE], jnp.where(main, 0.0, pick).astype(BF16), TN)
    dx_high += mm(recv_ref[:, TILE : 2 * TILE], jnp.where(main, 0.0, shift).astype(BF16), TN)
    dx_ref[:half, :] = (cot_ref[:half, :].astype(F32) + dx_low[:half]).astype(BF16)
    dx_ref[half:, :] = (cot_ref[half:, :].astype(F32) + dx_high[:half]).astype(BF16)


def exchange(rows, groups):
    parts = rows.reshape(groups, PAD, 3 * TILE)
    parts = lax.all_to_all(parts, "expert", split_axis=0, concat_axis=0, tiled=True)
    return parts.reshape(groups * PAD, 3 * TILE)


def body(tokens, cotangent, expert_ids, combine, w_up, w_down):
    toks, feat = tokens.shape
    groups = lax.axis_size("expert")
    hidden = w_up.shape[2]
    kept, padded = groups * CAP, groups * PAD
    shape = jax.ShapeDtypeStruct
    dma = pltpu.SemaphoreType.DMA
    tok, cot, ids, comb = tokens.T, cotangent.T, expert_ids.T, combine.T
    up, down = w_up[0], w_down[0].T
    weights = [pltpu.VMEM((feat, hidden), BF16)] * 2

    send, disp = call(
        dispatch_kernel,
        (shape((padded, 3 * TILE), BF16), shape((padded, 2 * toks), BF16)),
        (HBM, HBM),
        (ids, comb, tok, cot),
        [HBM] * 4,
        [pltpu.VMEM(a.shape, a.dtype) for a in (ids, comb, tok, cot)]
        + [pltpu.VMEM((padded, 3 * TILE), BF16), pltpu.VMEM((padded, 2 * toks), BF16), dma((4,)), dma((4,))],
    )
    recv = exchange(send, groups)
    pieces = tuple(shape((r.stop - r.start, c.stop - c.start), BF16) for r, c in places(kept, hidden))
    count = len(pieces)
    g_rows, *terms = call(
        functools.partial(up_kernel, count),
        (shape((kept, feat), BF16),) + 2 * pieces,
        (HBM,) * (1 + 2 * count),
        (recv, up, down),
        [HBM] * 3,
        [
            pltpu.VMEM((2, kept, hidden), BF16),
            pltpu.VMEM((padded, 3 * TILE), BF16),
            pltpu.VMEM((kept, feat), BF16),
            *weights,
            dma((3,)),
            dma((2 * count + 1,)),
        ],
    )
    sums = lax.psum(tuple(terms), "dp")
    send_back, act = call(
        functools.partial(down_kernel, count),
        (shape((padded, 3 * TILE), BF16), shape((kept, hidden), BF16)),
        (HBM, HBM),
        (*sums, up, down),
        [HBM] * (2 * count + 2),
        [
            pltpu.VMEM((2, kept, hidden), BF16),
            pltpu.VMEM((kept, hidden), BF16),
            pltpu.VMEM((kept, hidden), BF16),
            pltpu.VMEM((kept, TILE), F32),
            pltpu.VMEM((kept, 2 * TILE), F32),
            pltpu.VMEM((kept, 2 * TILE), F32),
            pltpu.VMEM((2 * TILE, hidden), BF16),
            pltpu.VMEM((2 * TILE, hidden), BF16),
            pltpu.VMEM((padded, 3 * TILE), BF16),
            dma((2 * count,)),
            dma((8,)),
        ],
    )
    back = exchange(send_back, groups)
    down_grad = call(grad_kernel, shape((feat, hidden), BF16), VMEM, (g_rows, act), [VMEM] * 2)
    layer_out, input_grad, combine_grad = call(
        combine_kernel,
        (shape((feat, toks), BF16), shape((feat, toks), BF16), shape((2, toks), F32)),
        (VMEM,) * 3,
        (back, disp, ids, comb, tok, cot),
        [VMEM] * 6,
        limit=8,
    )
    return layer_out.T, input_grad.T, combine_grad.T, down_grad.T[None]


def solution(mesh):
    in_specs = (
        P("expert", "dp"),
        P("expert", "dp"),
        P("expert", None),
        P("expert", None),
        P("expert", "dp", None),
        P("expert", None, "dp"),
    )
    out_specs = (P("expert", "dp"), P("expert", "dp"), P("expert", None), P("expert", None, "dp"))
    return jax.shard_map(body, mesh=mesh, in_specs=in_specs, out_specs=out_specs, check_vma=False)
```
